32 devices in a mesh: groups: 2 (over y), leaf: 4 (over z), cols: 2 (over x), sub: 2 (over core).
Axes of the slice: x: 2, y: 2, z: 4, core: 2. Of those that a mesh axis runs over, the one named last changes fastest.
Arguments:
- points: bfloat16 [128, 131072], P(('groups', 'cols'), ('leaf', 'sub')), parts along dimension 0, may hold values from -6 to 6
- leaf_basis: bfloat16 [512, 64, 256], P(('leaf', 'sub')), may hold values from -0.375 to 0.375
- transfer: bfloat16 [512, 64, 64], P(('leaf', 'sub')), may hold values from -0.5 to 0.5
- far_list: int32 [512, 8], P(('leaf', 'sub')), may hold values from -1 to 511, as said below
- far_coupling: bfloat16 [512, 64, 512], P(('leaf', 'sub')), may hold values from -0.25 to 0.25
- near_list: int32 [512, 5], P(('leaf', 'sub')), may hold values from -1 to 511, as said below
- near_blocks: bfloat16 [512, 5, 256, 256], P(('leaf', 'sub')), may hold values from -0.15625 to 0.15625
- top_coupling: bfloat16 [8, 64, 512], P(('leaf', 'sub')), may hold values from -0.1875 to 0.1875
Outputs:
- product: bfloat16 [128, 131072], P(('groups', 'cols'), ('leaf', 'sub')), parts along dimension 0
The draws below stay inside these ranges and needn't reach their ends.
There are 2 independent parts, one for each index of `groups`. The reference program is written for one: setup_inputs(seed, part) draws one part's arguments, and reference() takes and returns one part's arrays. A program takes and returns all parts, laid end to end along the dimension named above; an argument that names none is the same for every part. Nothing has to cross between parts.
Inputs may be any that keep to these rules, and one draw needn't show every extreme that they name: `near_list`: each row lists near-field boxes of that leaf box, -1 marking an empty slot; slot 0 holds the box itself, every listed box lies at most 4 boxes away, and no box is listed twice in a row. `far_list`: each row lists far-field partners of that leaf box, -1 marking an empty slot; every listed box lies more than 4 and at most 8 boxes away, and no box is listed twice in a row.
All inputs are finite; a program needn't handle non-finite values.
Results may differ from the reference program's by a relative error of at most 0.0057.
Values may be sent and summed in bfloat16 or wider, within the bound.
No kernel may reach another device: no remote copies, remote signals or barrier semaphores. Data moves between devices by JAX's collectives and lax.ppermute only.
A program may use at most 192 MiB of HBM per device.

```python
import jax
import jax.numpy as jnp
from jax import lax

RHS = 64
LEAF = 256
RANK = 64
BOX_DEV = 64
NNEAR = 5
NFAR = 8
REACH = 4
FREACH = 8
NDEV = 8
NBOX = 512
NPTS = 131072


def band_ids(key, lowest, highest, slots, least, with_self):
    box_ids = jnp.arange(NBOX, dtype=jnp.int32)
    inner_offsets = jnp.arange(lowest, highest, dtype=jnp.int32)
    offset_pool = jnp.concatenate([inner_offsets, -inner_offsets])
    pool_size = 2 * (highest - lowest)
    score_key, count_key = jax.random.split(key)
    scores = jax.random.randint(score_key, (NBOX, pool_size), 0, 4096, dtype=jnp.int32) * pool_size
    scores = scores + jnp.arange(pool_size, dtype=jnp.int32)[None, :]
    ranking = jnp.argsort(scores, axis=1, stable=True)
    picked = offset_pool[ranking]
    if with_self:
        leading_values = [0, highest, -highest]
    else:
        leading_values = [highest, -highest]
    leading = jnp.broadcast_to(jnp.array(leading_values, dtype=jnp.int32)[None, :], (NBOX, len(leading_values)))
    offsets = jnp.concatenate([leading, picked], axis=1)[:, :slots]
    counts = jax.random.randint(count_key, (NBOX, 1), least, slots + 1, dtype=jnp.int32)
    target = box_ids[:, None] + offsets
    keep = (jnp.arange(slots, dtype=jnp.int32)[None, :] < counts) & (target >= 0) & (target < NBOX)
    return jnp.where(keep, target, -1).astype(jnp.int32)


def draw_near_list(key, part):
    key = jax.random.fold_in(key, 11)
    return band_ids(key, 1, REACH, NNEAR, 3, True)


def draw_far_list(key, part):
    key = jax.random.fold_in(key, 23)
    return band_ids(key, REACH + 1, FREACH, NFAR, 4, False)


def steps_of(stream_key, extent, cuts, low, high):
    def one(axis_at, blocks):
        heights = jax.random.uniform(jax.random.fold_in(jax.random.fold_in(stream_key, 6), axis_at), (blocks,), jnp.float32, low / len(cuts), high / len(cuts))
        return jnp.repeat(jnp.exp(heights), extent[axis_at] // blocks).reshape((-1,) + (1,) * (len(extent) - axis_at - 1))

    gain = one(*cuts[0])
    for cut in cuts[1:]:
        gain = gain * one(*cut)
    return gain


def scatter_about(rng, shape, deviation, reach, pieces=(), held_as=jnp.bfloat16):
    values = jax.random.normal(rng, shape, jnp.float32) * deviation
    if len(pieces) > 0:
        values = steps_of(rng, shape, pieces, -0.22, 0.18) * values
    return jnp.clip(values, min=-reach, max=reach).astype(held_as)


def setup_inputs(seed: int = 0, part: int = 0) -> dict:
    key_of = jax.random.split(jax.random.key(seed), 9)
    part_splits = jax.random.split(jax.random.fold_in(key_of[8], part), 9)
    return {
        "points": scatter_about(part_splits[0], (RHS, NPTS), 1.0, 6.0, ((0, 2), (1, 8))),
        "leaf_basis": scatter_about(key_of[1], (NBOX, RANK, LEAF), LEAF ** -0.5, 0.375, ((0, 8),)),
        "transfer": scatter_about(key_of[2], (NBOX, RANK, RANK), (2 * RANK) ** -0.5, 0.5, ((0, 8),)),
        "far_list": draw_far_list(jax.random.fold_in(key_of[8], 71), part),
        "far_coupling": scatter_about(key_of[4], (NBOX, RANK, NFAR * RANK), (NFAR * RANK) ** -0.5, 0.25, ((0, 8),)),
        "near_list": draw_near_list(jax.random.fold_in(key_of[8], 71), part),
        "near_blocks": scatter_about(key_of[6], (NBOX, NNEAR, LEAF, LEAF), (NNEAR * LEAF) ** -0.5, 0.15625, ((0, 8),)),
        "top_coupling": scatter_about(key_of[7], (NDEV, RANK, NDEV * RANK), (16 * RANK) ** -0.5, 0.1875, ((0, 8),)),
    }


def reference(points, leaf_basis, transfer, far_list, far_coupling, near_list, near_blocks, top_coupling):
    single = jnp.float32
    point_boxes = points.reshape(RHS, NBOX, LEAF)
    coefficients = jnp.einsum('bkl,cbl->cbk', leaf_basis.astype(single), point_boxes.astype(single)).astype(jnp.bfloat16)
    grouped = coefficients.astype(single).reshape(RHS, NDEV, BOX_DEV, RANK)
    root_coeffs = jnp.einsum('cdbk,dbkp->cdp', grouped, transfer.astype(single).reshape(NDEV, BOX_DEV, RANK, RANK)).astype(jnp.bfloat16)
    owner = jnp.arange(NDEV * RANK, dtype=jnp.int32) // RANK
    device_ids = jnp.arange(NDEV, dtype=jnp.int32)
    distant = jnp.abs(owner[None, :] - device_ids[:, None]) >= 2
    top_weights = jnp.where(distant[:, None, :], top_coupling.astype(single), jnp.zeros((), single))
    top_sum = jnp.einsum('dkj,cj->cdk', top_weights, root_coeffs.reshape(RHS, NDEV * RANK).astype(single))
    box_top = jnp.repeat(top_sum, BOX_DEV, axis=1)
    downward = jnp.einsum('bkp,cbp->cbk', transfer.astype(single), box_top, precision=lax.Precision.HIGHEST)
    present = far_list >= 0
    held = jnp.take(coefficients, jnp.clip(far_list, 0, NBOX - 1), axis=1)
    held = jnp.where(present[None, :, :, None], held, jnp.zeros((), jnp.bfloat16))
    far_sum = jnp.einsum('bkj,cbj->cbk', far_coupling.astype(single), held.reshape(RHS, NBOX, NFAR * RANK).astype(single))
    coeff_out = (far_sum + downward).astype(jnp.bfloat16)
    far_points = jnp.einsum('bkl,cbk->cbl', leaf_basis.astype(single), coeff_out.astype(single))
    live = near_list >= 0
    nearby = jnp.take(point_boxes, jnp.clip(near_list, 0, NBOX - 1), axis=1)
    nearby = jnp.where(live[None, :, :, None], nearby, jnp.zeros((), jnp.bfloat16))
    near_sum = jnp.einsum('bjpl,cbjl->cbp', near_blocks.astype(single), nearby.astype(single))
    return (far_points + near_sum).astype(jnp.bfloat16).reshape(RHS, NPTS)
```

```python
import functools

import jax
import jax.numpy as jnp
from jax import lax
from jax.experimental import pallas as pl
from jax.experimental.pallas import tpu as pltpu
from jax.sharding import PartitionSpec as P

REACH = 4
FREACH = 8
SUBTREE = ("leaf", "sub")
F32 = jnp.float32
BF16 = jnp.bfloat16
LANES = 128
CHUNK = 8
ROWS_FIRST = 3


def dot(a, b, a_dim, b_dim):
    return lax.dot_general(a, b, (((a_dim,), (b_dim,)), ((), ())), preferred_element_type=F32)


def low_half(shape):
    return lax.broadcasted_iota(jnp.int32, shape, len(shape) - 1) < LANES // 2


def point_slice(box, leaf):
    return pl.ds(pl.multiple_of(box * leaf, leaf), leaf)


def near_box(blocks, extended, near_list, box, first_box, boxes, leaf, slots):
    moving = None
    fixed = None
    for slot in range(slots):
        listed = near_list[box, slot]
        place = jnp.where(listed < 0, boxes + 2 * REACH, listed - first_box + REACH)
        source = extended[:, point_slice(place, leaf)]
        if slot < ROWS_FIRST:
            term = dot(source, blocks[slot], 1, 1)
            moving = term if moving is None else moving + term
        else:
            term = dot(blocks[slot], source, 1, 1)
            fixed = term if fixed is None else fixed + term
    return moving + fixed.T


def up_kernel(rounds, place_ref, points, basis, transfer, coeffs, *rest):
    pays = rest[:rounds]
    flat, pts, bas, tra, sem = rest[rounds:]
    boxes, rank, leaf = basis.shape
    columns = points.shape[0]
    device = place_ref[0]
    parts = sem.shape[0] - 1
    per = boxes // parts
    copies = []
    for part in range(parts):
        copies.append(
            (
                pltpu.make_async_copy(
                    points.at[:, pl.ds(part * per * leaf, per * leaf)],
                    pts.at[:, pl.ds(part * per * leaf, per * leaf)],
                    sem.at[part, 0],
                ),
                pltpu.make_async_copy(
                    basis.at[pl.ds(part * per, per)], bas.at[pl.ds(part * per, per)], sem.at[part, 1]
                ),
            )
        )
    for a, b in copies:
        a.start()
        b.start()
    whole = pltpu.make_async_copy(transfer, tra, sem.at[parts, 0])
    whole.start()
    low = low_half((columns, LANES))
    for part in range(parts):
        for c in copies[part]:
            c.wait()
        for pair in range(part * per // 2, (part + 1) * per // 2):
            box = 2 * pair
            both = jnp.concatenate(
                [pts[:, box * leaf : (box + 1) * leaf], pts[:, (box + 1) * leaf : (box + 2) * leaf]], 0
            )
            grown = dot(both, bas[box : box + 2].reshape(2 * rank, leaf), 1, 1)
            joined = jnp.where(low, grown[:columns], grown[columns:])
            turned = pltpu.roll(joined, LANES // 2, 1)
            flat[:, box * rank : (box + 2) * rank] = joined.astype(BF16)
            coeffs[box] = jnp.where(low, joined, turned).astype(BF16)
            coeffs[box + 1] = jnp.where(low, turned, joined).astype(BF16)
    whole.wait()
    root = dot(flat[...], tra[...].reshape(boxes * rank, rank), 1, 0)
    root = jnp.concatenate([root, root], 1).astype(BF16)
    near_blocks = REACH * leaf // LANES
    far_blocks = FREACH * rank // LANES
    for step in range(rounds):
        upper = lax.rem(device, 2 << step) >= (1 << step)
        first = jnp.where(upper, 0, (boxes - REACH) * leaf)
        for i in range(near_blocks):
            pays[step][i] = pts[:, pl.ds(pl.multiple_of(first + i * LANES, LANES), LANES)]
        first = jnp.where(upper, 0, (boxes - FREACH) * rank)
        for i in range(far_blocks):
            pays[step][near_blocks + i] = flat[:, pl.ds(pl.multiple_of(first + i * LANES, LANES), LANES)]
        pays[step][near_blocks + far_blocks] = root


def near_kernel(place_ref, near_list, points, blocks, out, extended, buf, sem, psem):
    boxes, slots, leaf = blocks.shape[:3]
    columns = points.shape[0]
    first_box = place_ref[0] * boxes
    count = boxes - 2 * REACH
    chunks = count // CHUNK

    def chunk_copy(c):
        return pltpu.make_async_copy(
            blocks.at[pl.ds(REACH + c * CHUNK, CHUNK)], buf.at[pl.ds(c * CHUNK, CHUNK)], sem.at[c]
        )

    pcopy = pltpu.make_async_copy(
        points, extended.at[:, pl.ds(REACH * leaf, boxes * leaf)], psem
    )
    pcopy.start()
    for c in range(chunks):
        chunk_copy(c).start()
    extended[:, pl.ds((boxes + 2 * REACH) * leaf, leaf)] = jnp.zeros((columns, leaf), BF16)
    pcopy.wait()

    @pl.loop(0, chunks)
    def _(c):
        chunk_copy(c).wait()
        for i in range(CHUNK):
            at = c * CHUNK + i
            out[:, point_slice(at, leaf)] = near_box(
                buf.at[at], extended, near_list, at + REACH, first_box, boxes, leaf, slots
            )


def down_kernel(rounds, order, place_ref, near_list, far_list, *refs):
    points, coeffs, partial, basis, transfer, coupling, top, blocks, own = refs[:9]
    arrived = refs[9 : 9 + rounds]
    out = refs[9 + rounds]
    extended, wide, down, bas, tra, cou, buf, sem, ssem = refs[10 + rounds :]
    boxes, slots, leaf = blocks.shape[:3]
    rank = basis.shape[1]
    columns = points.shape[0]
    far_slots = far_list.shape[1]
    device = place_ref[0]
    first_box = device * boxes
    edge = 2 * REACH
    near_blocks = REACH * leaf // LANES
    far_blocks = FREACH * rank // LANES
    chunks = boxes // CHUNK

    pcopy = pltpu.make_async_copy(points, extended.at[:, pl.ds(REACH * leaf, boxes * leaf)], ssem.at[0])
    ccopy = pltpu.make_async_copy(coeffs, wide.at[pl.ds(FREACH, boxes)], ssem.at[1])
    tcopy = pltpu.make_async_copy(transfer, tra, ssem.at[2])
    lowcopy = pltpu.make_async_copy(blocks.at[pl.ds(0, REACH)], buf.at[pl.ds(0, REACH)], ssem.at[3])
    highcopy = pltpu.make_async_copy(
        blocks.at[pl.ds(boxes - REACH, REACH)], buf.at[pl.ds(REACH, REACH)], ssem.at[4]
    )

    def chunk_copy(c):
        here = pl.ds(c * CHUNK, CHUNK)
        return (
            pltpu.make_async_copy(coupling.at[here], cou.at[here], sem.at[c, 0]),
            pltpu.make_async_copy(basis.at[here], bas.at[here], sem.at[c, 1]),
        )

    tcopy.start()
    ccopy.start()
    pcopy.start()
    lowcopy.start()
    for c in range(chunks):
        for copy in chunk_copy(c):
            copy.start()
    highcopy.start()

    low = low_half((columns, LANES))
    roots = [own[0]]
    for step in range(rounds):
        for i in range(1 << step):
            roots.append(arrived[step][near_blocks + far_blocks + i])
    lane = lax.broadcasted_iota(jnp.int32, (columns, LANES), 1)
    total = jnp.zeros((columns, rank), F32)
    for i in range(0, len(order), 2):
        owner = jnp.bitwise_xor(device, order[i])
        odd = lax.rem(owner, 2)
        even_owner = owner - odd
        both = jnp.where(lane // (LANES // 2) == odd, roots[i], roots[i + 1])
        owners = even_owner + lane // (LANES // 2)
        both = jnp.where(jnp.abs(owners - device) >= 2, both, jnp.zeros((), BF16))
        weights = top[0, :, pl.ds(pl.multiple_of(even_owner * rank, 2 * rank), 2 * rank)]
        total = total + dot(both, weights, 1, 1)
    high_part = total.astype(BF16)
    rest = (total - high_part.astype(F32)).astype(BF16)
    both = jnp.concatenate([high_part, rest], 0)

    extended[:, pl.ds((boxes + 2 * REACH) * leaf, leaf)] = jnp.zeros((columns, leaf), BF16)
    wide[boxes + 2 * FREACH] = jnp.zeros((columns, LANES), BF16)
    for step in range(rounds):
        place = lax.rem(device, 2 << step)
        for half in range(2):

            @pl.when(place == (1 << step) - 1 + half)
            def _(step=step, half=half):
                first = 0 if half else boxes + REACH
                for i in range(near_blocks):
                    extended[:, first * leaf + i * LANES : first * leaf + (i + 1) * LANES] = arrived[step][i]
                first = 0 if half else boxes + FREACH
                for i in range(far_blocks):
                    joined = arrived[step][near_blocks + i].astype(F32)
                    turned = pltpu.roll(joined, LANES // 2, 1)
                    wide[first + 2 * i] = jnp.where(low, joined, turned).astype(BF16)
                    wide[first + 2 * i + 1] = jnp.where(low, turned, joined).astype(BF16)

    tcopy.wait()
    grown = dot(both, tra[...].reshape(boxes * rank, rank), 1, 1)
    down[...] = grown[:columns] + grown[columns:]
    ccopy.wait()
    pcopy.wait()
    lowcopy.wait()
    row = lax.broadcasted_iota(jnp.int32, (2 * columns, LANES), 0)
    lane2 = lax.broadcasted_iota(jnp.int32, (2 * columns, LANES), 1)
    low2 = row // columns == lane2 // (LANES // 2)

    def one_pair(pair, near):
        box = 2 * pair
        held = []
        for side in range(2):
            pieces = []
            for slot in range(0, far_slots, 2):
                taken = []
                for s in range(2):
                    listed = far_list[box + side, slot + s]
                    place = jnp.where(listed < 0, boxes + 2 * FREACH, listed - first_box + FREACH)
                    taken.append(wide[place])
                pieces.append(jnp.where(low, taken[0], taken[1]))
            held.append(jnp.concatenate(pieces, 1))
        here = pl.ds(box, 2)
        far = dot(jnp.concatenate(held, 0), cou[here].reshape(2 * rank, far_slots * rank), 1, 1)
        far = jnp.where(low, far[:columns], far[columns:])
        far = far + down[:, pl.ds(pl.multiple_of(pair * LANES, LANES), LANES)]
        far = far.astype(BF16)
        spread = jnp.where(low2, jnp.concatenate([far, far], 0), jnp.zeros((), BF16))
        spread = dot(spread, bas[here].reshape(2 * rank, leaf), 1, 0)
        for side in range(2):
            out[:, point_slice(box + side, leaf)] = (
                spread[side * columns : (side + 1) * columns] + near(box + side)
            ).astype(BF16)

    def from_partial(box):
        return partial[:, point_slice(box - REACH, leaf)]

    def from_blocks(box):
        at = box if box < REACH else box - boxes + edge
        return near_box(buf.at[at], extended, near_list, box, first_box, boxes, leaf, slots)

    for c in range(chunks):
        for copy in chunk_copy(c):
            copy.wait()
        if c == chunks - 1:
            highcopy.wait()
        for pair in range(c * CHUNK // 2, (c + 1) * CHUNK // 2):
            box = 2 * pair
            inner = REACH <= box < boxes - REACH
            one_pair(pair, from_partial if inner else from_blocks)


def shards(
    points, leaf_basis, transfer, far_list, far_coupling, near_list, near_blocks, top_coupling
):
    columns = points.shape[0]
    boxes, rank, leaf = leaf_basis.shape
    slots = near_list.shape[1]
    size = lax.axis_size("leaf") * lax.axis_size("sub")
    rounds = size.bit_length() - 1
    device = lax.axis_index(SUBTREE)
    place = device[None].astype(jnp.int32)
    hbm = pl.BlockSpec(memory_space=pl.ANY)
    vmem = pl.BlockSpec(memory_space=pltpu.VMEM)
    smem = pl.BlockSpec(memory_space=pltpu.SMEM)
    params = pltpu.CompilerParams(vmem_limit_bytes=56 * 2**20)
    halo = REACH * leaf // LANES + FREACH * rank // LANES

    parts = 4
    outs = pl.pallas_call(
        functools.partial(up_kernel, rounds),
        out_shape=[jax.ShapeDtypeStruct((boxes, columns, LANES), BF16)]
        + [jax.ShapeDtypeStruct((halo + (1 << k), columns, LANES), BF16) for k in range(rounds)],
        in_specs=[smem, hbm, hbm, hbm],
        out_specs=[vmem] * (1 + rounds),
        scratch_shapes=[
            pltpu.VMEM((columns, boxes * rank), BF16),
            pltpu.VMEM((columns, boxes * leaf), BF16),
            pltpu.VMEM((boxes, rank, leaf), BF16),
            pltpu.VMEM((boxes, rank, rank), BF16),
            pltpu.SemaphoreType.DMA((parts + 1, 2)),
        ],
        compiler_params=params,
        name="upward",
    )(place, points, leaf_basis, transfer)
    coeffs, pays = outs[0], list(outs[1:])
    own = pays[0][halo : halo + 1]

    arrived = []
    order = [0]
    for step in range(rounds):
        flip = (2 << step) - 1
        got = lax.ppermute(pays[step], SUBTREE, [(i, i ^ flip) for i in range(size)])
        arrived.append(got)
        for later in range(step + 1, rounds):
            pays[later] = lax.dynamic_update_slice_in_dim(
                pays[later], got[halo:], halo + (1 << step), axis=0
            )
        order = order + [flip ^ o for o in order]

    inner = boxes - 2 * REACH
    span = boxes + 2 * REACH + 1
    partial = pl.pallas_call(
        near_kernel,
        out_shape=jax.ShapeDtypeStruct((columns, inner * leaf), F32),
        in_specs=[smem, smem, hbm, hbm],
        out_specs=vmem,
        scratch_shapes=[
            pltpu.VMEM((columns, span * leaf), BF16),
            pltpu.VMEM((inner, slots, leaf, leaf), BF16),
            pltpu.SemaphoreType.DMA((inner // CHUNK,)),
            pltpu.SemaphoreType.DMA(()),
        ],
        compiler_params=params,
        cost_estimate=pl.CostEstimate(
            flops=2 * columns * inner * slots * leaf * leaf,
            bytes_accessed=2 * inner * slots * leaf * leaf,
            transcendentals=0,
        ),
        name="near_inner",
    )(place, near_list, points, near_blocks)

    product = pl.pallas_call(
        functools.partial(down_kernel, rounds, order),
        out_shape=jax.ShapeDtypeStruct((columns, boxes * leaf), BF16),
        in_specs=[smem, smem, smem, hbm, hbm, vmem, hbm, hbm, hbm, vmem, hbm, vmem] + [vmem] * rounds,
        out_specs=vmem,
        scratch_shapes=[
            pltpu.VMEM((columns, span * leaf), BF16),
            pltpu.VMEM((boxes + 2 * FREACH + 1, columns, LANES), BF16),
            pltpu.VMEM((columns, boxes * rank), F32),
            pltpu.VMEM((boxes, rank, leaf), BF16),
            pltpu.VMEM((boxes, rank, rank), BF16),
            pltpu.VMEM(far_coupling.shape, BF16),
            pltpu.VMEM((2 * REACH, slots, leaf, leaf), BF16),
            pltpu.SemaphoreType.DMA((boxes // CHUNK, 2)),
            pltpu.SemaphoreType.DMA((5,)),
        ],
        compiler_params=params,
        name="downward",
    )(
        place, near_list, far_list, points, coeffs, partial, leaf_basis, transfer, far_coupling,
        top_coupling, near_blocks, own, *arrived,
    )
    return product


def solution(mesh):
    in_specs = (
        P(("groups", "cols"), SUBTREE),
        P(SUBTREE, None, None),
        P(SUBTREE, None, None),
        P(SUBTREE, None),
        P(SUBTREE, None, None),
        P(SUBTREE, None),
        P(SUBTREE, None, None, None),
        P(SUBTREE, None, None),
    )
    out_specs = P(("groups", "cols"), SUBTREE)
    return jax.shard_map(shards, mesh=mesh, in_specs=in_specs, out_specs=out_specs, check_vma=False)
```

```python
import functools

import jax
import jax.numpy as jnp
from jax import lax
from jax.experimental import pallas as pl
from jax.experimental.pallas import tpu as pltpu
from jax.sharding import PartitionSpec as P

REACH = 4
FREACH = 8
SUBTREE = ("leaf", "sub")
F32 = jnp.float32
BF16 = jnp.bfloat16
LANES = 128
CHUNK = 8
AHEAD = 2
UP_VMEM = 3
UP_COST = 2 * 10**10
MOVING = 3


def dot(a, b, a_dim, b_dim):
    return lax.dot_general(a, b, (((a_dim,), (b_dim,)), ((), ())), preferred_element_type=F32)


def low_half(shape):
    return lax.broadcasted_iota(jnp.int32, shape, len(shape) - 1) < LANES // 2


def point_slice(box, leaf):
    return pl.ds(pl.multiple_of(box * leaf, leaf), leaf)


def spread_pair(joined):
    low = low_half(joined.shape)
    turned = pltpu.roll(joined, LANES // 2, 1)
    return jnp.where(low, joined, turned).astype(BF16), jnp.where(low, turned, joined).astype(BF16)


def near_box(blocks, held, near_list, box, base, empty, leaf):
    moving = None
    fixed = None
    for slot in range(blocks.shape[0]):
        listed = near_list[slot, box]
        place = jnp.where(listed < 0, empty, listed - base)
        source = held[:, point_slice(place, leaf)]
        if slot < MOVING:
            term = dot(source, blocks[slot], 1, 1)
            moving = term if moving is None else moving + term
        else:
            term = dot(blocks[slot], source, 1, 1)
            fixed = term if fixed is None else fixed + term
    return moving + fixed.T


def up_kernel(place_ref, points, basis, transfer, pts, bas, tra, coeffs, inner, outer, flat, sem):
    boxes, rank, leaf = basis.shape
    columns = points.shape[0]
    device = place_ref[0]
    parts = sem.shape[0] - 1
    per = boxes // parts
    copies = []
    for part in range(parts):
        lanes = pl.ds(part * per * leaf, per * leaf)
        here = pl.ds(part * per, per)
        copies.append(
            (
                pltpu.make_async_copy(points.at[:, lanes], pts.at[:, lanes], sem.at[part, 0]),
                pltpu.make_async_copy(basis.at[here], bas.at[here], sem.at[part, 1]),
            )
        )
    whole = pltpu.make_async_copy(transfer, tra, sem.at[parts, 0])
    for a, b in copies:
        a.start()
        b.start()
    whole.start()
    pts[:, boxes * leaf :] = jnp.zeros((columns, leaf), BF16)
    coeffs[boxes] = jnp.zeros((columns, LANES), BF16)
    low = low_half((columns, LANES))
    for part in range(parts):
        for c in copies[part]:
            c.wait()
        for box in range(part * per, (part + 1) * per, 2):
            both = jnp.concatenate(
                [pts[:, box * leaf : (box + 1) * leaf], pts[:, (box + 1) * leaf : (box + 2) * leaf]], 0
            )
            grown = dot(both, bas[box : box + 2].reshape(2 * rank, leaf), 1, 1)
            joined = jnp.where(low, grown[:columns], grown[columns:])
            flat[:, box * rank : (box + 2) * rank] = joined.astype(BF16)
            coeffs[box], coeffs[box + 1] = spread_pair(joined)
    whole.wait()
    root = dot(flat[...], tra[...].reshape(boxes * rank, rank), 1, 0)
    root = jnp.concatenate([root, root], 1).astype(BF16)
    near_blocks = REACH * leaf // LANES
    far_blocks = FREACH * rank // LANES
    odd = lax.rem(device, 2)
    for pay, at_start in ((inner, odd), (outer, 1 - odd)):
        first = jnp.where(at_start == 1, 0, (boxes - REACH) * leaf)
        for i in range(near_blocks):
            pay[i] = pts[:, pl.ds(pl.multiple_of(first + i * LANES, LANES), LANES)]
        first = jnp.where(at_start == 1, 0, (boxes - FREACH) * rank)
        for i in range(far_blocks):
            pay[near_blocks + i] = flat[:, pl.ds(pl.multiple_of(first + i * LANES, LANES), LANES)]
    inner[near_blocks + far_blocks] = root


def down_kernel(order, place_ref, near_list, far_list, *refs):
    pts, coeffs, basis, transfer, coupling, top, blocks, roots, inner, outer, out = refs[:11]
    edge_pts, edge_coeffs, stage, sem, out_sem = refs[11:]
    boxes, slots, leaf = blocks.shape[:3]
    rank = basis.shape[1]
    columns = pts.shape[0]
    far_slots = far_list.shape[0]
    device = place_ref[0]
    base = device * boxes
    near_blocks = REACH * leaf // LANES
    far_blocks = FREACH * rank // LANES
    chunks = boxes // CHUNK

    def in_copy(c):
        here = pl.ds(c * CHUNK, CHUNK)
        return pltpu.make_async_copy(coupling.at[here], cou.at[here], sem.at[c])

    def out_copy(c):
        lanes = pl.ds(c * CHUNK * leaf, CHUNK * leaf)
        return pltpu.make_async_copy(stage.at[:, lanes], out.at[:, lanes], out_sem.at[c])


    low = low_half((columns, LANES))
    lane = lax.broadcasted_iota(jnp.int32, (columns, LANES), 1)
    total = jnp.zeros((columns, rank), F32)
    for i in range(0, len(order), 2):
        owner = jnp.bitwise_xor(device, order[i])
        odd = lax.rem(owner, 2)
        even_owner = owner - odd
        both = jnp.where(lane // (LANES // 2) == odd, roots[i], roots[i + 1])
        owners = even_owner + lane // (LANES // 2)
        both = jnp.where(jnp.abs(owners - device) >= 2, both, jnp.zeros((), BF16))
        weights = top[0, :, pl.ds(pl.multiple_of(even_owner * rank, 2 * rank), 2 * rank)]
        total = total + dot(both, weights, 1, 1)
    high_part = total.astype(BF16)
    rest = (total - high_part.astype(F32)).astype(BF16)
    top_parts = jnp.concatenate([high_part, rest], 0)

    near_span = CHUNK + 2 * REACH
    far_span = CHUNK + 2 * FREACH
    near_first = (-REACH, boxes - CHUNK - REACH)
    far_first = (-FREACH, boxes - CHUNK - FREACH)
    for edge in range(2):
        skip = (1 - edge) * REACH
        first = near_first[edge] + skip
        edge_pts[edge, :, skip * leaf : (skip + CHUNK + REACH) * leaf] = pts[
            :, first * leaf : (first + CHUNK + REACH) * leaf
        ]
        edge_pts[edge, :, near_span * leaf :] = jnp.zeros((columns, leaf), BF16)
        skip = (1 - edge) * FREACH
        first = far_first[edge] + skip
        edge_coeffs[edge, skip : skip + CHUNK + FREACH] = coeffs[first : first + CHUNK + FREACH]
        edge_coeffs[edge, far_span] = jnp.zeros((columns, LANES), BF16)

    def halo(edge, source):
        first = edge * (CHUNK + REACH) * leaf
        for i in range(near_blocks):
            edge_pts[edge, :, first + i * LANES : first + (i + 1) * LANES] = source[i]
        first = edge * (CHUNK + FREACH)
        for i in range(far_blocks):
            even, odd = spread_pair(source[near_blocks + i].astype(F32))
            edge_coeffs[edge, first + 2 * i] = even
            edge_coeffs[edge, first + 2 * i + 1] = odd

    @pl.when(lax.rem(device, 2) == 0)
    def _():
        halo(0, outer)
        halo(1, inner)

    @pl.when(lax.rem(device, 2) == 1)
    def _():
        halo(0, inner)
        halo(1, outer)

    row = lax.broadcasted_iota(jnp.int32, (2 * columns, LANES), 0)
    lane2 = lax.broadcasted_iota(jnp.int32, (2 * columns, LANES), 1)
    own_half = row // columns == lane2 // (LANES // 2)

    for c in range(chunks):
        if c == 0 or c == chunks - 1:
            edge = 0 if c == 0 else 1
            near_held, near_base, near_empty = edge_pts.at[edge], base + near_first[edge], near_span
            far_held, far_base, far_empty = edge_coeffs.at[edge], base + far_first[edge], far_span
        else:
            near_held, near_base, near_empty = pts, base, boxes
            far_held, far_base, far_empty = coeffs, base, boxes
        first = c * CHUNK
        down = dot(top_parts, transfer[first : first + CHUNK].reshape(CHUNK * rank, rank), 1, 1)
        down = down[:columns] + down[columns:]
        fars = []
        for pair in range(CHUNK // 2):
            rows = []
            for side in range(2):
                box = first + 2 * pair + side
                pieces = []
                for slot in range(0, far_slots, 2):
                    taken = []
                    for s in range(2):
                        listed = far_list[slot + s, box]
                        taken.append(far_held[jnp.where(listed < 0, far_empty, listed - far_base)])
                    pieces.append(jnp.where(low, taken[0], taken[1]))
                rows.append(jnp.concatenate(pieces, 1))
            box = first + 2 * pair
            weights = coupling[box : box + 2].reshape(2 * rank, far_slots * rank)
            fars.append(dot(jnp.concatenate(rows, 0), weights, 1, 1))
        nears = [
            near_box(blocks.at[first + i], near_held, near_list, first + i, near_base, near_empty, leaf)
            for i in range(CHUNK)
        ]
        for pair in range(CHUNK // 2):
            box = first + 2 * pair
            far = jnp.where(low, fars[pair][:columns], fars[pair][columns:])
            far = (far + down[:, pair * LANES : (pair + 1) * LANES]).astype(BF16)
            spread = jnp.where(own_half, jnp.concatenate([far, far], 0), jnp.zeros((), BF16))
            spread = dot(spread, basis[box : box + 2].reshape(2 * rank, leaf), 1, 0)
            for side in range(2):
                stage[:, (box + side) * leaf : (box + side + 1) * leaf] = (
                    spread[side * columns : (side + 1) * columns] + nears[2 * pair + side]
                ).astype(BF16)
        out_copy(c).start()
    for c in range(chunks):
        out_copy(c).wait()


def in_vmem(x):
    return pltpu.with_memory_space_constraint(x, pltpu.VMEM)


def in_hbm(x):
    return pltpu.with_memory_space_constraint(x, pltpu.HBM)


def shards(
    points, leaf_basis, transfer, far_list, far_coupling, near_list, near_blocks, top_coupling
):
    columns = points.shape[0]
    boxes, rank, leaf = leaf_basis.shape
    size = lax.axis_size("leaf") * lax.axis_size("sub")
    rounds = size.bit_length() - 1
    device = lax.axis_index(SUBTREE)
    place = device[None].astype(jnp.int32)
    hbm = pl.BlockSpec(memory_space=pl.ANY)
    vmem = pl.BlockSpec(memory_space=pltpu.VMEM)
    smem = pl.BlockSpec(memory_space=pltpu.SMEM)
    halo = REACH * leaf // LANES + FREACH * rank // LANES

    parts = 4
    pts, bas, tra, coeffs, inner, outer = pl.pallas_call(
        up_kernel,
        out_shape=[
            pltpu.VMEM((columns, (boxes + 1) * leaf), BF16),
            pltpu.VMEM((boxes, rank, leaf), BF16),
            pltpu.VMEM((boxes, rank, rank), BF16),
            pltpu.VMEM((boxes + 1, columns, LANES), BF16),
            pltpu.VMEM((halo + 1, columns, LANES), BF16),
            pltpu.VMEM((halo, columns, LANES), BF16),
        ],
        in_specs=[smem, hbm, hbm, hbm],
        out_specs=[vmem] * 6,
        scratch_shapes=[
            pltpu.VMEM((columns, boxes * rank), BF16),
            pltpu.SemaphoreType.DMA((parts + 1, 2)),
        ],
        compiler_params=pltpu.CompilerParams(vmem_limit_bytes=UP_VMEM * 2**20),
        cost_estimate=pl.CostEstimate(flops=UP_COST, bytes_accessed=2 * boxes * rank * leaf, transcendentals=0),
        name="upward",
    )(place, in_hbm(points), in_hbm(leaf_basis), in_hbm(transfer))

    inner_got = lax.ppermute(inner, SUBTREE, [(i, i ^ 1) for i in range(size)])
    outer_pairs = [(i, i + 1) for i in range(1, size - 1, 2)]
    outer_got = lax.ppermute(outer, SUBTREE, outer_pairs + [(j, i) for i, j in outer_pairs])
    roots = jnp.concatenate([inner[halo:], inner_got[halo:]], 0)
    order = [0, 1]
    for step in range(1, rounds):
        if step == rounds - 1:
            roots, outer_got = lax.optimization_barrier((roots, outer_got))
        flip = (2 << step) - 1
        got = lax.ppermute(roots, SUBTREE, [(i, i ^ flip) for i in range(size)])
        roots = jnp.concatenate([roots, got], 0)
        order = order + [flip ^ o for o in order]

    far = far_coupling
    held = [pts, coeffs, bas, tra, far_coupling, top_coupling, near_blocks, roots, inner_got, outer_got]
    placed = [in_vmem(x) for x in held]
    return pl.pallas_call(
        functools.partial(down_kernel, order),
        out_shape=jax.ShapeDtypeStruct((columns, boxes * leaf), BF16),
        in_specs=[smem, smem, smem] + [vmem for x in held],
        out_specs=hbm,
        scratch_shapes=[
            pltpu.VMEM((2, columns, (CHUNK + 2 * REACH + 1) * leaf), BF16),
            pltpu.VMEM((2, CHUNK + 2 * FREACH + 1, columns, LANES), BF16),
            pltpu.VMEM((columns, boxes * leaf), BF16),
            pltpu.SemaphoreType.DMA((boxes // CHUNK,)),
            pltpu.SemaphoreType.DMA((boxes // CHUNK,)),
        ],
        compiler_params=pltpu.CompilerParams(vmem_limit_bytes=4 * 2**20),
        name="downward",
    )(place, near_list.T, far_list.T, *placed)


def solution(mesh):
    in_specs = (
        P(("groups", "cols"), SUBTREE),
        P(SUBTREE, None, None),
        P(SUBTREE, None, None),
        P(SUBTREE, None),
        P(SUBTREE, None, None),
        P(SUBTREE, None),
        P(SUBTREE, None, None, None),
        P(SUBTREE, None, None),
    )
    out_specs = P(("groups", "cols"), SUBTREE)
    return jax.shard_map(shards, mesh=mesh, in_specs=in_specs, out_specs=out_specs, check_vma=False)
```

```python
import functools

import jax
import jax.numpy as jnp
from jax import lax
from jax.experimental import pallas as pl
from jax.experimental.pallas import tpu as pltpu
from jax.sharding import PartitionSpec as P

REACH = 4
FREACH = 8
SUBTREE = ("leaf", "sub")
F32 = jnp.float32
BF16 = jnp.bfloat16
LANES = 128
CHUNK = 8
UP_VMEM = 3
UP_COST = 2 * 10**10
MOVING = 2


def dot(a, b, a_dim, b_dim):
    return lax.dot_general(a, b, (((a_dim,), (b_dim,)), ((), ())), preferred_element_type=F32)


def low_half(shape):
    return lax.broadcasted_iota(jnp.int32, shape, len(shape) - 1) < LANES // 2


def point_slice(box, leaf):
    return pl.ds(pl.multiple_of(box * leaf, leaf), leaf)


def spread_pair(joined):
    low = low_half(joined.shape)
    turned = pltpu.roll(joined, LANES // 2, 1)
    return jnp.where(low, joined, turned).astype(BF16), jnp.where(low, turned, joined).astype(BF16)


def near_box(blocks, held, near_list, box, base, empty, leaf):
    moving = None
    fixed = None
    for slot in range(blocks.shape[0]):
        listed = near_list[slot, box]
        place = jnp.where(listed < 0, empty, listed - base)
        source = held[:, point_slice(place, leaf)]
        if slot < MOVING:
            term = dot(source, blocks[slot], 1, 1)
            moving = term if moving is None else moving + term
        else:
            term = dot(blocks[slot], source, 1, 1)
            fixed = term if fixed is None else fixed + term
    return moving + fixed.T


def up_kernel(place_ref, points, basis, transfer, pts, bas, tra, coeffs, inner, outer, flat, sem):
    boxes, rank, leaf = basis.shape
    columns = points.shape[0]
    device = place_ref[0]
    parts = sem.shape[0] - 1
    per = boxes // parts
    copies = []
    for part in range(parts):
        lanes = pl.ds(part * per * leaf, per * leaf)
        here = pl.ds(part * per, per)
        copies.append(
            (
                pltpu.make_async_copy(points.at[:, lanes], pts.at[:, lanes], sem.at[part, 0]),
                pltpu.make_async_copy(basis.at[here], bas.at[here], sem.at[part, 1]),
            )
        )
    whole = pltpu.make_async_copy(transfer, tra, sem.at[parts, 0])
    for a, b in copies:
        a.start()
        b.start()
    whole.start()
    pts[:, boxes * leaf :] = jnp.zeros((columns, leaf), BF16)
    coeffs[boxes] = jnp.zeros((columns, LANES), BF16)
    low = low_half((columns, LANES))
    for part in range(parts):
        for c in copies[part]:
            c.wait()
        for box in range(part * per, (part + 1) * per, 2):
            both = jnp.concatenate(
                [pts[:, box * leaf : (box + 1) * leaf], pts[:, (box + 1) * leaf : (box + 2) * leaf]], 0
            )
            grown = dot(both, bas[box : box + 2].reshape(2 * rank, leaf), 1, 1)
            joined = jnp.where(low, grown[:columns], grown[columns:])
            flat[:, box * rank : (box + 2) * rank] = joined.astype(BF16)
            coeffs[box], coeffs[box + 1] = spread_pair(joined)
    whole.wait()
    root = dot(flat[...], tra[...].reshape(boxes * rank, rank), 1, 0)
    root = jnp.concatenate([root, root], 1).astype(BF16)
    near_blocks = REACH * leaf // LANES
    far_blocks = FREACH * rank // LANES
    odd = lax.rem(device, 2)
    for pay, at_start in ((inner, odd), (outer, 1 - odd)):
        first = jnp.where(at_start == 1, 0, (boxes - REACH) * leaf)
        for i in range(near_blocks):
            pay[i] = pts[:, pl.ds(pl.multiple_of(first + i * LANES, LANES), LANES)]
        first = jnp.where(at_start == 1, 0, (boxes - FREACH) * rank)
        for i in range(far_blocks):
            pay[near_blocks + i] = flat[:, pl.ds(pl.multiple_of(first + i * LANES, LANES), LANES)]
    inner[near_blocks + far_blocks] = root


def down_kernel(order, place_ref, near_list, far_list, *refs):
    pts, coeffs, basis, transfer, coupling, top, blocks, roots, inner, outer, out = refs[:11]
    edge_pts, edge_coeffs, stage, out_sem = refs[11:]
    boxes, slots, leaf = blocks.shape[:3]
    rank = basis.shape[1]
    columns = pts.shape[0]
    far_slots = far_list.shape[0]
    device = place_ref[0]
    base = device * boxes
    near_blocks = REACH * leaf // LANES
    far_blocks = FREACH * rank // LANES
    chunks = boxes // CHUNK

    def out_copy(c):
        lanes = pl.ds(c * CHUNK * leaf, CHUNK * leaf)
        return pltpu.make_async_copy(stage.at[:, lanes], out.at[:, lanes], out_sem.at[c])


    low = low_half((columns, LANES))
    lane = lax.broadcasted_iota(jnp.int32, (columns, LANES), 1)
    total = jnp.zeros((columns, rank), F32)
    for i in range(0, len(order), 2):
        owner = jnp.bitwise_xor(device, order[i])
        odd = lax.rem(owner, 2)
        even_owner = owner - odd
        both = jnp.where(lane // (LANES // 2) == odd, roots[i], roots[i + 1])
        owners = even_owner + lane // (LANES // 2)
        both = jnp.where(jnp.abs(owners - device) >= 2, both, jnp.zeros((), BF16))
        weights = top[0, :, pl.ds(pl.multiple_of(even_owner * rank, 2 * rank), 2 * rank)]
        total = total + dot(both, weights, 1, 1)
    high_part = total.astype(BF16)
    rest = (total - high_part.astype(F32)).astype(BF16)
    top_parts = jnp.concatenate([high_part, rest], 0)

    near_span = CHUNK + 2 * REACH
    far_span = CHUNK + 2 * FREACH
    near_first = (-REACH, boxes - CHUNK - REACH)
    far_first = (-FREACH, boxes - CHUNK - FREACH)
    for edge in range(2):
        skip = (1 - edge) * REACH
        first = near_first[edge] + skip
        edge_pts[edge, :, skip * leaf : (skip + CHUNK + REACH) * leaf] = pts[
            :, first * leaf : (first + CHUNK + REACH) * leaf
        ]
        edge_pts[edge, :, near_span * leaf :] = jnp.zeros((columns, leaf), BF16)
        skip = (1 - edge) * FREACH
        first = far_first[edge] + skip
        edge_coeffs[edge, skip : skip + CHUNK + FREACH] = coeffs[first : first + CHUNK + FREACH]
        edge_coeffs[edge, far_span] = jnp.zeros((columns, LANES), BF16)

    def halo(edge, source):
        first = edge * (CHUNK + REACH) * leaf
        for i in range(near_blocks):
            edge_pts[edge, :, first + i * LANES : first + (i + 1) * LANES] = source[i]
        first = edge * (CHUNK + FREACH)
        for i in range(far_blocks):
            even, odd = spread_pair(source[near_blocks + i].astype(F32))
            edge_coeffs[edge, first + 2 * i] = even
            edge_coeffs[edge, first + 2 * i + 1] = odd

    @pl.when(lax.rem(device, 2) == 0)
    def _():
        halo(0, outer)
        halo(1, inner)

    @pl.when(lax.rem(device, 2) == 1)
    def _():
        halo(0, inner)
        halo(1, outer)

    row = lax.broadcasted_iota(jnp.int32, (2 * columns, LANES), 0)
    lane2 = lax.broadcasted_iota(jnp.int32, (2 * columns, LANES), 1)
    own_half = row // columns == lane2 // (LANES // 2)

    for c in range(chunks):
        if c == 0 or c == chunks - 1:
            edge = 0 if c == 0 else 1
            near_held, near_base, near_empty = edge_pts.at[edge], base + near_first[edge], near_span
            far_held, far_base, far_empty = edge_coeffs.at[edge], base + far_first[edge], far_span
        else:
            near_held, near_base, near_empty = pts, base, boxes
            far_held, far_base, far_empty = coeffs, base, boxes
        first = c * CHUNK
        down = dot(top_parts, transfer[first : first + CHUNK].reshape(CHUNK * rank, rank), 1, 1)
        down = down[:columns] + down[columns:]
        fars = []
        for pair in range(CHUNK // 2):
            rows = []
            for side in range(2):
                box = first + 2 * pair + side
                pieces = []
                for slot in range(0, far_slots, 2):
                    taken = []
                    for s in range(2):
                        listed = far_list[slot + s, box]
                        taken.append(far_held[jnp.where(listed < 0, far_empty, listed - far_base)])
                    pieces.append(jnp.where(low, taken[0], taken[1]))
                rows.append(jnp.concatenate(pieces, 1))
            box = first + 2 * pair
            weights = coupling[box : box + 2].reshape(2 * rank, far_slots * rank)
            fars.append(dot(jnp.concatenate(rows, 0), weights, 1, 1))
        nears = [
            near_box(blocks.at[first + i], near_held, near_list, first + i, near_base, near_empty, leaf)
            for i in range(CHUNK)
        ]
        for pair in range(CHUNK // 2):
            box = first + 2 * pair
            far = jnp.where(low, fars[pair][:columns], fars[pair][columns:])
            far = (far + down[:, pair * LANES : (pair + 1) * LANES]).astype(BF16)
            spread = jnp.where(own_half, jnp.concatenate([far, far], 0), jnp.zeros((), BF16))
            spread = dot(spread, basis[box : box + 2].reshape(2 * rank, leaf), 1, 0)
            for side in range(2):
                stage[:, (box + side) * leaf : (box + side + 1) * leaf] = (
                    spread[side * columns : (side + 1) * columns] + nears[2 * pair + side]
                ).astype(BF16)
        out_copy(c).start()
    for c in range(chunks):
        out_copy(c).wait()


def in_vmem(x):
    return pltpu.with_memory_space_constraint(x, pltpu.VMEM)


def in_hbm(x):
    return pltpu.with_memory_space_constraint(x, pltpu.HBM)


def shards(
    points, leaf_basis, transfer, far_list, far_coupling, near_list, near_blocks, top_coupling
):
    columns = points.shape[0]
    boxes, rank, leaf = leaf_basis.shape
    size = lax.axis_size("leaf") * lax.axis_size("sub")
    rounds = size.bit_length() - 1
    device = lax.axis_index(SUBTREE)
    place = device[None].astype(jnp.int32)
    hbm = pl.BlockSpec(memory_space=pl.ANY)
    vmem = pl.BlockSpec(memory_space=pltpu.VMEM)
    smem = pl.BlockSpec(memory_space=pltpu.SMEM)
    halo = REACH * leaf // LANES + FREACH * rank // LANES

    parts = 4
    pts, bas, tra, coeffs, inner, outer = pl.pallas_call(
        up_kernel,
        out_shape=[
            pltpu.VMEM((columns, (boxes + 1) * leaf), BF16),
            pltpu.VMEM((boxes, rank, leaf), BF16),
            pltpu.VMEM((boxes, rank, rank), BF16),
            pltpu.VMEM((boxes + 1, columns, LANES), BF16),
            pltpu.VMEM((halo + 1, columns, LANES), BF16),
            pltpu.VMEM((halo, columns, LANES), BF16),
        ],
        in_specs=[smem, hbm, hbm, hbm],
        out_specs=[vmem] * 6,
        scratch_shapes=[
            pltpu.VMEM((columns, boxes * rank), BF16),
            pltpu.SemaphoreType.DMA((parts + 1, 2)),
        ],
        compiler_params=pltpu.CompilerParams(vmem_limit_bytes=UP_VMEM * 2**20),
        cost_estimate=pl.CostEstimate(flops=UP_COST, bytes_accessed=2 * boxes * rank * leaf, transcendentals=0),
        name="upward",
    )(place, in_hbm(points), in_hbm(leaf_basis), in_hbm(transfer))

    inner_got = lax.ppermute(inner, SUBTREE, [(i, i ^ 1) for i in range(size)])
    outer_pairs = [(i, i + 1) for i in range(1, size - 1, 2)]
    outer_got = lax.ppermute(outer, SUBTREE, outer_pairs + [(j, i) for i, j in outer_pairs])
    roots = jnp.concatenate([inner[halo:], inner_got[halo:]], 0)
    order = [0, 1]
    for step in range(1, rounds):
        flip = 1 << step
        got = lax.ppermute(roots, SUBTREE, [(i, i ^ flip) for i in range(size)])
        roots = jnp.concatenate([roots, got], 0)
        order = order + [flip ^ o for o in order]

    held = [pts, coeffs, bas, tra, far_coupling, top_coupling, near_blocks, roots, inner_got, outer_got]
    placed = [in_vmem(x) for x in held]
    return pl.pallas_call(
        functools.partial(down_kernel, order),
        out_shape=jax.ShapeDtypeStruct((columns, boxes * leaf), BF16),
        in_specs=[smem, smem, smem] + [vmem for x in held],
        out_specs=hbm,
        scratch_shapes=[
            pltpu.VMEM((2, columns, (CHUNK + 2 * REACH + 1) * leaf), BF16),
            pltpu.VMEM((2, CHUNK + 2 * FREACH + 1, columns, LANES), BF16),
            pltpu.VMEM((columns, boxes * leaf), BF16),
            pltpu.SemaphoreType.DMA((boxes // CHUNK,)),
        ],
        compiler_params=pltpu.CompilerParams(vmem_limit_bytes=4 * 2**20),
        name="downward",
    )(place, near_list.T, far_list.T, *placed)


def solution(mesh):
    in_specs = (
        P(("groups", "cols"), SUBTREE),
        P(SUBTREE, None, None),
        P(SUBTREE, None, None),
        P(SUBTREE, None),
        P(SUBTREE, None, None),
        P(SUBTREE, None),
        P(SUBTREE, None, None, None),
        P(SUBTREE, None, None),
    )
    out_specs = P(("groups", "cols"), SUBTREE)
    return jax.shard_map(shards, mesh=mesh, in_specs=in_specs, out_specs=out_specs, check_vma=False)
```

```python
import functools

import jax
import jax.numpy as jnp
from jax import lax
from jax.experimental import pallas as pl
from jax.experimental.pallas import tpu as pltpu
from jax.sharding import PartitionSpec as P

REACH = 4
FREACH = 8
SUBTREE = ("leaf", "sub")
F32 = jnp.float32
BF16 = jnp.bfloat16
LANES = 128
CHUNK = 8
UP_VMEM = 3
UP_COST = 2 * 10**10
MOVING = 2


def dot(a, b, a_dim, b_dim):
    return lax.dot_general(a, b, (((a_dim,), (b_dim,)), ((), ())), preferred_element_type=F32)


def low_half(shape):
    return lax.broadcasted_iota(jnp.int32, shape, len(shape) - 1) < LANES // 2


def point_slice(box, leaf):
    return pl.ds(pl.multiple_of(box * leaf, leaf), leaf)


def spread_pair(joined):
    low = low_half(joined.shape)
    turned = pltpu.roll(joined, LANES // 2, 1)
    return jnp.where(low, joined, turned).astype(BF16), jnp.where(low, turned, joined).astype(BF16)


def near_box(blocks, held, near_list, box, base, empty, leaf):
    moving = None
    fixed = None
    for slot in range(blocks.shape[0]):
        listed = near_list[slot, box]
        place = jnp.where(listed < 0, empty, listed - base)
        source = held[:, point_slice(place, leaf)]
        if slot < MOVING:
            term = dot(source, blocks[slot], 1, 1)
            moving = term if moving is None else moving + term
        else:
            term = dot(blocks[slot], source, 1, 1)
            fixed = term if fixed is None else fixed + term
    return moving + fixed.T


def up_kernel(place_ref, points, basis, transfer, pts, bas, tra, coeffs, inner, outer, flat, sem):
    boxes, rank, leaf = basis.shape
    columns = points.shape[0]
    device = place_ref[0]
    parts = sem.shape[0] - 1
    per = boxes // parts
    copies = []
    for part in range(parts):
        lanes = pl.ds(part * per * leaf, per * leaf)
        here = pl.ds(part * per, per)
        copies.append(
            (
                pltpu.make_async_copy(points.at[:, lanes], pts.at[:, lanes], sem.at[part, 0]),
                pltpu.make_async_copy(basis.at[here], bas.at[here], sem.at[part, 1]),
            )
        )
    whole = pltpu.make_async_copy(transfer, tra, sem.at[parts, 0])
    for a, b in copies:
        a.start()
        b.start()
    whole.start()
    pts[:, boxes * leaf :] = jnp.zeros((columns, leaf), BF16)
    coeffs[boxes] = jnp.zeros((columns, LANES), BF16)
    low = low_half((columns, LANES))
    for part in range(parts):
        for c in copies[part]:
            c.wait()
        for box in range(part * per, (part + 1) * per, 2):
            both = jnp.concatenate(
                [pts[:, box * leaf : (box + 1) * leaf], pts[:, (box + 1) * leaf : (box + 2) * leaf]], 0
            )
            grown = dot(both, bas[box : box + 2].reshape(2 * rank, leaf), 1, 1)
            joined = jnp.where(low, grown[:columns], grown[columns:])
            flat[:, box * rank : (box + 2) * rank] = joined.astype(BF16)
            coeffs[box], coeffs[box + 1] = spread_pair(joined)
    whole.wait()
    root = dot(flat[...], tra[...].reshape(boxes * rank, rank), 1, 0)
    root = jnp.concatenate([root, root], 1).astype(BF16)
    near_blocks = REACH * leaf // LANES
    far_blocks = FREACH * rank // LANES
    odd = lax.rem(device, 2)
    for pay, at_start in ((inner, odd), (outer, 1 - odd)):
        first = jnp.where(at_start == 1, 0, (boxes - REACH) * leaf)
        for i in range(near_blocks):
            pay[i] = pts[:, pl.ds(pl.multiple_of(first + i * LANES, LANES), LANES)]
        first = jnp.where(at_start == 1, 0, (boxes - FREACH) * rank)
        for i in range(far_blocks):
            pay[near_blocks + i] = flat[:, pl.ds(pl.multiple_of(first + i * LANES, LANES), LANES)]
    inner[near_blocks + far_blocks] = root


def down_kernel(order, place_ref, near_list, far_list, *refs):
    pts, coeffs, basis, transfer, coupling, top, blocks, roots, inner, outer, out = refs[:11]
    edge_pts, edge_coeffs, stage, out_sem = refs[11:]
    boxes, slots, leaf = blocks.shape[:3]
    rank = basis.shape[1]
    columns = pts.shape[0]
    far_slots = far_list.shape[0]
    device = place_ref[0]
    base = device * boxes
    near_blocks = REACH * leaf // LANES
    far_blocks = FREACH * rank // LANES
    chunks = boxes // CHUNK

    def out_copy(c):
        lanes = pl.ds(c * CHUNK * leaf, CHUNK * leaf)
        return pltpu.make_async_copy(stage.at[:, lanes], out.at[:, lanes], out_sem.at[c])


    low = low_half((columns, LANES))
    lane = lax.broadcasted_iota(jnp.int32, (columns, LANES), 1)
    total = jnp.zeros((columns, rank), F32)
    for i in range(0, len(order), 2):
        owner = jnp.bitwise_xor(device, order[i])
        odd = lax.rem(owner, 2)
        even_owner = owner - odd
        both = jnp.where(lane // (LANES // 2) == odd, roots[i], roots[i + 1])
        owners = even_owner + lane // (LANES // 2)
        both = jnp.where(jnp.abs(owners - device) >= 2, both, jnp.zeros((), BF16))
        weights = top[0, :, pl.ds(pl.multiple_of(even_owner * rank, 2 * rank), 2 * rank)]
        total = total + dot(both, weights, 1, 1)
    high_part = total.astype(BF16)
    rest = (total - high_part.astype(F32)).astype(BF16)
    top_parts = jnp.concatenate([high_part, rest], 0)

    near_span = CHUNK + 2 * REACH
    far_span = CHUNK + 2 * FREACH
    near_first = (-REACH, boxes - CHUNK - REACH)
    far_first = (-FREACH, boxes - CHUNK - FREACH)
    for edge in range(2):
        skip = (1 - edge) * REACH
        first = near_first[edge] + skip
        edge_pts[edge, :, skip * leaf : (skip + CHUNK + REACH) * leaf] = pts[
            :, first * leaf : (first + CHUNK + REACH) * leaf
        ]
        edge_pts[edge, :, near_span * leaf :] = jnp.zeros((columns, leaf), BF16)
        skip = (1 - edge) * FREACH
        first = far_first[edge] + skip
        edge_coeffs[edge, skip : skip + CHUNK + FREACH] = coeffs[first : first + CHUNK + FREACH]
        edge_coeffs[edge, far_span] = jnp.zeros((columns, LANES), BF16)

    def halo(edge, source):
        first = edge * (CHUNK + REACH) * leaf
        for i in range(near_blocks):
            edge_pts[edge, :, first + i * LANES : first + (i + 1) * LANES] = source[i]
        first = edge * (CHUNK + FREACH)
        for i in range(far_blocks):
            even, odd = spread_pair(source[near_blocks + i].astype(F32))
            edge_coeffs[edge, first + 2 * i] = even
            edge_coeffs[edge, first + 2 * i + 1] = odd

    @pl.when(lax.rem(device, 2) == 0)
    def _():
        halo(0, outer)
        halo(1, inner)

    @pl.when(lax.rem(device, 2) == 1)
    def _():
        halo(0, inner)
        halo(1, outer)

    row = lax.broadcasted_iota(jnp.int32, (2 * columns, LANES), 0)
    lane2 = lax.broadcasted_iota(jnp.int32, (2 * columns, LANES), 1)
    own_half = row // columns == lane2 // (LANES // 2)

    for c in range(chunks):
        if c == 0 or c == chunks - 1:
            edge = 0 if c == 0 else 1
            near_held, near_base, near_empty = edge_pts.at[edge], base + near_first[edge], near_span
            far_held, far_base, far_empty = edge_coeffs.at[edge], base + far_first[edge], far_span
        else:
            near_held, near_base, near_empty = pts, base, boxes
            far_held, far_base, far_empty = coeffs, base, boxes
        first = c * CHUNK
        down = dot(top_parts, transfer[first : first + CHUNK].reshape(CHUNK * rank, rank), 1, 1)
        down = down[:columns] + down[columns:]
        fars = []
        for pair in range(CHUNK // 2):
            rows = []
            for side in range(2):
                box = first + 2 * pair + side
                pieces = []
                for slot in range(0, far_slots, 2):
                    taken = []
                    for s in range(2):
                        listed = far_list[slot + s, box]
                        taken.append(far_held[jnp.where(listed < 0, far_empty, listed - far_base)])
                    pieces.append(jnp.where(low, taken[0], taken[1]))
                rows.append(jnp.concatenate(pieces, 1))
            box = first + 2 * pair
            weights = coupling[box : box + 2].reshape(2 * rank, far_slots * rank)
            fars.append(dot(jnp.concatenate(rows, 0), weights, 1, 1))
        nears = [
            near_box(blocks.at[first + i], near_held, near_list, first + i, near_base, near_empty, leaf)
            for i in range(CHUNK)
        ]
        for pair in range(CHUNK // 2):
            box = first + 2 * pair
            far = jnp.where(low, fars[pair][:columns], fars[pair][columns:])
            far = (far + down[:, pair * LANES : (pair + 1) * LANES]).astype(BF16)
            spread = jnp.where(own_half, jnp.concatenate([far, far], 0), jnp.zeros((), BF16))
            spread = dot(spread, basis[box : box + 2].reshape(2 * rank, leaf), 1, 0)
            for side in range(2):
                stage[:, (box + side) * leaf : (box + side + 1) * leaf] = (
                    spread[side * columns : (side + 1) * columns] + nears[2 * pair + side]
                ).astype(BF16)
        out_copy(c).start()
    for c in range(chunks):
        out_copy(c).wait()


def in_vmem(x):
    return pltpu.with_memory_space_constraint(x, pltpu.VMEM)


def in_hbm(x):
    return pltpu.with_memory_space_constraint(x, pltpu.HBM)


def shards(
    points, leaf_basis, transfer, far_list, far_coupling, near_list, near_blocks, top_coupling
):
    columns = points.shape[0]
    boxes, rank, leaf = leaf_basis.shape
    size = lax.axis_size("leaf") * lax.axis_size("sub")
    rounds = size.bit_length() - 1
    device = lax.axis_index(SUBTREE)
    place = device[None].astype(jnp.int32)
    hbm = pl.BlockSpec(memory_space=pl.ANY)
    vmem = pl.BlockSpec(memory_space=pltpu.VMEM)
    smem = pl.BlockSpec(memory_space=pltpu.SMEM)
    halo = REACH * leaf // LANES + FREACH * rank // LANES

    parts = 2
    pts, bas, tra, coeffs, inner, outer = pl.pallas_call(
        up_kernel,
        out_shape=[
            pltpu.VMEM((columns, (boxes + 1) * leaf), BF16),
            pltpu.VMEM((boxes, rank, leaf), BF16),
            pltpu.VMEM((boxes, rank, rank), BF16),
            pltpu.VMEM((boxes + 1, columns, LANES), BF16),
            pltpu.VMEM((halo + 1, columns, LANES), BF16),
            pltpu.VMEM((halo, columns, LANES), BF16),
        ],
        in_specs=[smem, hbm, hbm, hbm],
        out_specs=[vmem] * 6,
        scratch_shapes=[
            pltpu.VMEM((columns, boxes * rank), BF16),
            pltpu.SemaphoreType.DMA((parts + 1, 2)),
        ],
        compiler_params=pltpu.CompilerParams(vmem_limit_bytes=UP_VMEM * 2**20),
        cost_estimate=pl.CostEstimate(flops=UP_COST, bytes_accessed=2 * boxes * rank * leaf, transcendentals=0),
        name="upward",
    )(place, in_hbm(points), in_hbm(leaf_basis), in_hbm(transfer))

    inner_got = lax.ppermute(inner, SUBTREE, [(i, i ^ 1) for i in range(size)])
    outer_pairs = [(i, i + 1) for i in range(1, size - 1, 2)]
    outer_got = lax.ppermute(outer, SUBTREE, outer_pairs + [(j, i) for i, j in outer_pairs])
    roots = jnp.concatenate([inner[halo:], inner_got[halo:]], 0)
    order = [0, 1]
    for step in range(1, rounds):
        flip = size >> step
        got = lax.ppermute(roots, SUBTREE, [(i, i ^ flip) for i in range(size)])
        roots = jnp.concatenate([roots, got], 0)
        order = order + [flip ^ o for o in order]

    held = [pts, coeffs, bas, tra, far_coupling, top_coupling, near_blocks, roots, inner_got, outer_got]
    placed = [in_vmem(x) for x in held]
    return pl.pallas_call(
        functools.partial(down_kernel, order),
        out_shape=jax.ShapeDtypeStruct((columns, boxes * leaf), BF16),
        in_specs=[smem, smem, smem] + [vmem for x in held],
        out_specs=hbm,
        scratch_shapes=[
            pltpu.VMEM((2, columns, (CHUNK + 2 * REACH + 1) * leaf), BF16),
            pltpu.VMEM((2, CHUNK + 2 * FREACH + 1, columns, LANES), BF16),
            pltpu.VMEM((columns, boxes * leaf), BF16),
            pltpu.SemaphoreType.DMA((boxes // CHUNK,)),
        ],
        compiler_params=pltpu.CompilerParams(vmem_limit_bytes=4 * 2**20),
        name="downward",
    )(place, near_list.T, far_list.T, *placed)


def solution(mesh):
    in_specs = (
        P(("groups", "cols"), SUBTREE),
        P(SUBTREE, None, None),
        P(SUBTREE, None, None),
        P(SUBTREE, None),
        P(SUBTREE, None, None),
        P(SUBTREE, None),
        P(SUBTREE, None, None, None),
        P(SUBTREE, None, None),
    )
    out_specs = P(("groups", "cols"), SUBTREE)
    return jax.shard_map(shards, mesh=mesh, in_specs=in_specs, out_specs=out_specs, check_vma=False)
```

```python
import functools

import jax
import jax.numpy as jnp
from jax import lax
from jax.experimental import pallas as pl
from jax.experimental.pallas import tpu as pltpu
from jax.sharding import PartitionSpec as P

REACH = 4
FREACH = 8
SUBTREE = ("leaf", "sub")
F32 = jnp.float32
BF16 = jnp.bfloat16
LANES = 128
CHUNK = 8
UP_VMEM = 3
UP_COST = 2 * 10**10
MOVING = 2


def dot(a, b, a_dim, b_dim):
    return lax.dot_general(a, b, (((a_dim,), (b_dim,)), ((), ())), preferred_element_type=F32)


def low_half(shape):
    return lax.broadcasted_iota(jnp.int32, shape, len(shape) - 1) < LANES // 2


def point_slice(box, leaf):
    return pl.ds(pl.multiple_of(box * leaf, leaf), leaf)


def spread_pair(joined):
    low = low_half(joined.shape)
    turned = pltpu.roll(joined, LANES // 2, 1)
    return jnp.where(low, joined, turned).astype(BF16), jnp.where(low, turned, joined).astype(BF16)


def near_box(blocks, held, near_list, box, base, empty, leaf):
    moving = None
    fixed = None
    for slot in range(blocks.shape[0]):
        listed = near_list[slot, box]
        place = jnp.where(listed < 0, empty, listed - base)
        source = held[:, point_slice(place, leaf)]
        if slot < MOVING:
            term = dot(source, blocks[slot], 1, 1)
            moving = term if moving is None else moving + term
        else:
            term = dot(blocks[slot], source, 1, 1)
            fixed = term if fixed is None else fixed + term
    return moving + fixed.T


def up_kernel(place_ref, points, basis, transfer, pts, bas, tra, coeffs, inner, outer, flat, sem):
    boxes, rank, leaf = basis.shape
    columns = points.shape[0]
    device = place_ref[0]
    parts = sem.shape[0] - 1
    per = boxes // parts
    copies = []
    for part in range(parts):
        lanes = pl.ds(part * per * leaf, per * leaf)
        here = pl.ds(part * per, per)
        copies.append(
            (
                pltpu.make_async_copy(points.at[:, lanes], pts.at[:, lanes], sem.at[part, 0]),
                pltpu.make_async_copy(basis.at[here], bas.at[here], sem.at[part, 1]),
            )
        )
    whole = pltpu.make_async_copy(transfer, tra, sem.at[parts, 0])
    for a, b in copies:
        a.start()
        b.start()
    whole.start()
    pts[:, boxes * leaf :] = jnp.zeros((columns, leaf), BF16)
    coeffs[boxes] = jnp.zeros((columns, LANES), BF16)
    low = low_half((columns, LANES))
    for part in range(parts):
        for c in copies[part]:
            c.wait()
        for box in range(part * per, (part + 1) * per, 2):
            both = jnp.concatenate(
                [pts[:, box * leaf : (box + 1) * leaf], pts[:, (box + 1) * leaf : (box + 2) * leaf]], 0
            )
            grown = dot(both, bas[box : box + 2].reshape(2 * rank, leaf), 1, 1)
            joined = jnp.where(low, grown[:columns], grown[columns:])
            flat[:, box * rank : (box + 2) * rank] = joined.astype(BF16)
            coeffs[box], coeffs[box + 1] = spread_pair(joined)
    whole.wait()
    root = dot(flat[...], tra[...].reshape(boxes * rank, rank), 1, 0)
    root = jnp.concatenate([root, root], 1).astype(BF16)
    near_blocks = REACH * leaf // LANES
    far_blocks = FREACH * rank // LANES
    odd = lax.rem(device, 2)
    for pay, at_start in ((inner, odd), (outer, 1 - odd)):
        first = jnp.where(at_start == 1, 0, (boxes - REACH) * leaf)
        for i in range(near_blocks):
            pay[i] = pts[:, pl.ds(pl.multiple_of(first + i * LANES, LANES), LANES)]
        first = jnp.where(at_start == 1, 0, (boxes - FREACH) * rank)
        for i in range(far_blocks):
            pay[near_blocks + i] = flat[:, pl.ds(pl.multiple_of(first + i * LANES, LANES), LANES)]
    inner[near_blocks + far_blocks] = root


def down_kernel(order, place_ref, near_list, far_list, *refs):
    pts, coeffs, basis, transfer, coupling, top, blocks, roots, inner, outer, out = refs[:11]
    edge_pts, edge_coeffs, stage, out_sem = refs[11:]
    boxes, slots, leaf = blocks.shape[:3]
    rank = basis.shape[1]
    columns = pts.shape[0]
    far_slots = far_list.shape[0]
    device = place_ref[0]
    base = device * boxes
    near_blocks = REACH * leaf // LANES
    far_blocks = FREACH * rank // LANES
    chunks = boxes // CHUNK

    def out_copy(c):
        lanes = pl.ds(c * CHUNK * leaf, CHUNK * leaf)
        return pltpu.make_async_copy(stage.at[:, lanes], out.at[:, lanes], out_sem.at[c])


    low = low_half((columns, LANES))
    lane = lax.broadcasted_iota(jnp.int32, (columns, LANES), 1)
    total = jnp.zeros((columns, rank), F32)
    for i in range(0, len(order), 2):
        owner = jnp.bitwise_xor(device, order[i])
        odd = lax.rem(owner, 2)
        even_owner = owner - odd
        both = jnp.where(lane // (LANES // 2) == odd, roots[i], roots[i + 1])
        owners = even_owner + lane // (LANES // 2)
        both = jnp.where(jnp.abs(owners - device) >= 2, both, jnp.zeros((), BF16))
        weights = top[0, :, pl.ds(pl.multiple_of(even_owner * rank, 2 * rank), 2 * rank)]
        total = total + dot(both, weights, 1, 1)
    high_part = total.astype(BF16)
    rest = (total - high_part.astype(F32)).astype(BF16)
    top_parts = jnp.concatenate([high_part, rest], 0)

    near_span = CHUNK + 2 * REACH
    far_span = CHUNK + 2 * FREACH
    near_first = (-REACH, boxes - CHUNK - REACH)
    far_first = (-FREACH, boxes - CHUNK - FREACH)
    for edge in range(2):
        skip = (1 - edge) * REACH
        first = near_first[edge] + skip
        edge_pts[edge, :, skip * leaf : (skip + CHUNK + REACH) * leaf] = pts[
            :, first * leaf : (first + CHUNK + REACH) * leaf
        ]
        edge_pts[edge, :, near_span * leaf :] = jnp.zeros((columns, leaf), BF16)
        skip = (1 - edge) * FREACH
        first = far_first[edge] + skip
        edge_coeffs[edge, skip : skip + CHUNK + FREACH] = coeffs[first : first + CHUNK + FREACH]
        edge_coeffs[edge, far_span] = jnp.zeros((columns, LANES), BF16)

    def halo(edge, source):
        first = edge * (CHUNK + REACH) * leaf
        for i in range(near_blocks):
            edge_pts[edge, :, first + i * LANES : first + (i + 1) * LANES] = source[i]
        first = edge * (CHUNK + FREACH)
        for i in range(far_blocks):
            even, odd = spread_pair(source[near_blocks + i].astype(F32))
            edge_coeffs[edge, first + 2 * i] = even
            edge_coeffs[edge, first + 2 * i + 1] = odd

    @pl.when(lax.rem(device, 2) == 0)
    def _():
        halo(0, outer)
        halo(1, inner)

    @pl.when(lax.rem(device, 2) == 1)
    def _():
        halo(0, inner)
        halo(1, outer)

    row = lax.broadcasted_iota(jnp.int32, (2 * columns, LANES), 0)
    lane2 = lax.broadcasted_iota(jnp.int32, (2 * columns, LANES), 1)
    own_half = row // columns == lane2 // (LANES // 2)

    for c in range(chunks):
        if c == 0 or c == chunks - 1:
            edge = 0 if c == 0 else 1
            near_held, near_base, near_empty = edge_pts.at[edge], base + near_first[edge], near_span
            far_held, far_base, far_empty = edge_coeffs.at[edge], base + far_first[edge], far_span
        else:
            near_held, near_base, near_empty = pts, base, boxes
            far_held, far_base, far_empty = coeffs, base, boxes
        first = c * CHUNK
        down = dot(top_parts, transfer[first : first + CHUNK].reshape(CHUNK * rank, rank), 1, 1)
        down = down[:columns] + down[columns:]
        fars = []
        for pair in range(CHUNK // 2):
            rows = []
            for side in range(2):
                box = first + 2 * pair + side
                pieces = []
                for slot in range(0, far_slots, 2):
                    taken = []
                    for s in range(2):
                        listed = far_list[slot + s, box]
                        taken.append(far_held[jnp.where(listed < 0, far_empty, listed - far_base)])
                    pieces.append(jnp.where(low, taken[0], taken[1]))
                rows.append(jnp.concatenate(pieces, 1))
            box = first + 2 * pair
            weights = coupling[box : box + 2].reshape(2 * rank, far_slots * rank)
            fars.append(dot(jnp.concatenate(rows, 0), weights, 1, 1))
        nears = [
            near_box(blocks.at[first + i], near_held, near_list, first + i, near_base, near_empty, leaf)
            for i in range(CHUNK)
        ]
        for pair in range(CHUNK // 2):
            box = first + 2 * pair
            far = jnp.where(low, fars[pair][:columns], fars[pair][columns:])
            far = (far + down[:, pair * LANES : (pair + 1) * LANES]).astype(BF16)
            spread = jnp.where(own_half, jnp.concatenate([far, far], 0), jnp.zeros((), BF16))
            spread = dot(spread, basis[box : box + 2].reshape(2 * rank, leaf), 1, 0)
            for side in range(2):
                stage[:, (box + side) * leaf : (box + side + 1) * leaf] = (
                    spread[side * columns : (side + 1) * columns] + nears[2 * pair + side]
                ).astype(BF16)
        out_copy(c).start()
    for c in range(chunks):
        out_copy(c).wait()


def in_vmem(x):
    return pltpu.with_memory_space_constraint(x, pltpu.VMEM)


def in_hbm(x):
    return pltpu.with_memory_space_constraint(x, pltpu.HBM)


def shards(
    points, leaf_basis, transfer, far_list, far_coupling, near_list, near_blocks, top_coupling
):
    columns = points.shape[0]
    boxes, rank, leaf = leaf_basis.shape
    size = lax.axis_size("leaf") * lax.axis_size("sub")
    rounds = size.bit_length() - 1
    device = lax.axis_index(SUBTREE)
    place = device[None].astype(jnp.int32)
    hbm = pl.BlockSpec(memory_space=pl.ANY)
    vmem = pl.BlockSpec(memory_space=pltpu.VMEM)
    smem = pl.BlockSpec(memory_space=pltpu.SMEM)
    halo = REACH * leaf // LANES + FREACH * rank // LANES

    parts = 2
    pts, bas, tra, coeffs, inner, outer = pl.pallas_call(
        up_kernel,
        out_shape=[
            pltpu.VMEM((columns, (boxes + 1) * leaf), BF16),
            pltpu.VMEM((boxes, rank, leaf), BF16),
            pltpu.VMEM((boxes, rank, rank), BF16),
            pltpu.VMEM((boxes + 1, columns, LANES), BF16),
            pltpu.VMEM((halo + 1, columns, LANES), BF16),
            pltpu.VMEM((halo, columns, LANES), BF16),
        ],
        in_specs=[smem, hbm, hbm, hbm],
        out_specs=[vmem] * 6,
        scratch_shapes=[
            pltpu.VMEM((columns, boxes * rank), BF16),
            pltpu.SemaphoreType.DMA((parts + 1, 2)),
        ],
        compiler_params=pltpu.CompilerParams(vmem_limit_bytes=UP_VMEM * 2**20),
        cost_estimate=pl.CostEstimate(flops=UP_COST, bytes_accessed=2 * boxes * rank * leaf, transcendentals=0),
        name="upward",
    )(place, in_hbm(points), in_hbm(leaf_basis), in_hbm(transfer))

    inner_got = lax.ppermute(inner, SUBTREE, [(i, i ^ 1) for i in range(size)])
    outer_pairs = [(i, i + 1) for i in range(1, size - 1, 2)]
    outer_got = lax.ppermute(outer, SUBTREE, outer_pairs + [(j, i) for i, j in outer_pairs])
    roots = jnp.concatenate([inner[halo:], inner_got[halo:]], 0)
    order = [0, 1]
    for step in range(1, rounds):
        if step == rounds - 1:
            roots, outer_got = lax.optimization_barrier((roots, outer_got))
        flip = size >> step
        got = lax.ppermute(roots, SUBTREE, [(i, i ^ flip) for i in range(size)])
        roots = jnp.concatenate([roots, got], 0)
        order = order + [flip ^ o for o in order]

    held = [pts, coeffs, bas, tra, far_coupling, top_coupling, near_blocks, roots, inner_got, outer_got]
    placed = [in_vmem(x) for x in held]
    return pl.pallas_call(
        functools.partial(down_kernel, order),
        out_shape=jax.ShapeDtypeStruct((columns, boxes * leaf), BF16),
        in_specs=[smem, smem, smem] + [vmem for x in held],
        out_specs=hbm,
        scratch_shapes=[
            pltpu.VMEM((2, columns, (CHUNK + 2 * REACH + 1) * leaf), BF16),
            pltpu.VMEM((2, CHUNK + 2 * FREACH + 1, columns, LANES), BF16),
            pltpu.VMEM((columns, boxes * leaf), BF16),
            pltpu.SemaphoreType.DMA((boxes // CHUNK,)),
        ],
        compiler_params=pltpu.CompilerParams(vmem_limit_bytes=4 * 2**20),
        name="downward",
    )(place, near_list.T, far_list.T, *placed)


def solution(mesh):
    in_specs = (
        P(("groups", "cols"), SUBTREE),
        P(SUBTREE, None, None),
        P(SUBTREE, None, None),
        P(SUBTREE, None),
        P(SUBTREE, None, None),
        P(SUBTREE, None),
        P(SUBTREE, None, None, None),
        P(SUBTREE, None, None),
    )
    out_specs = P(("groups", "cols"), SUBTREE)
    return jax.shard_map(shards, mesh=mesh, in_specs=in_specs, out_specs=out_specs, check_vma=False)
```
